512 devices in a mesh: row: 16 (over z_lo, x), col: 32 (over z_hi, y, core).
Axes of the slice: x: 4, y: 4, z: 16 (z_hi: 4, z_lo: 4; z = z_hi * 4 + z_lo), core: 2. Of those that a mesh axis runs over, the one named last changes fastest.
Arguments:
- left_points: float32 [32768, 128], P(('row', 'col')), may hold values from -3.3 to 3.3
- right_points: float32 [32768, 128], P(('row', 'col')), may hold values from -3.3 to 3.3
- left_cotangent: bfloat16 [32768, 128], P(('row', 'col')), may hold values from -6 to 6
- right_coefficient: bfloat16 [32768, 128], P(('row', 'col')), may hold values from -6 to 6
Outputs:
- left_final: float32 [32768, 128], P(('row', 'col'))
- right_final: float32 [32768, 128], P(('row', 'col'))
- left_grad: float32 [32768, 128], P(('row', 'col'))
- right_grad: float32 [32768, 128], P(('row', 'col'))
The draws below stay inside these ranges and needn't reach their ends.
All inputs are finite; a program needn't handle non-finite values.
Results may differ from the reference program's by a relative error of at most 0.019.
Values may be sent and summed in bfloat16 or wider, within the bound.
A program may use at most 64 MiB of HBM per device.

```python
import jax
import jax.numpy as jnp
from jax import lax

F = 128
R = 128
PTS_DEV = 64
STEPS = 2
N = 32768
N_ROW = 16
N_COL = 32


def cluster_centers(key):
    center_key = jax.random.fold_in(key, 7001)
    center_scale = 0.6
    centers = jax.random.truncated_normal(center_key, -3.0, 3.0, (N_ROW * N_COL, F), jnp.float32)
    return centers * center_scale


def point_noise(key, salt):
    noise_key = jax.random.fold_in(key, salt)
    noise_scale = (32.0 / F) ** 0.5
    noise = jax.random.truncated_normal(noise_key, -3.0, 3.0, (N, F), jnp.float32)
    return noise * noise_scale


def draw_left_points(key, part):
    centers = cluster_centers(key)
    shuffled = jax.random.permutation(jax.random.fold_in(key, 7004), N).astype(jnp.int32)
    partner = shuffled % (N_ROW * N_COL)
    return centers[partner] + point_noise(key, 7002)


def draw_right_points(key, part):
    centers = cluster_centers(key)
    position = jnp.arange(N, dtype=jnp.int32)
    device = position // PTS_DEV
    return centers[device] + point_noise(key, 7003)


def shard_levels(own_key, dims, shards, low, top_value):
    def one(dim, blocks):
        draws = jax.random.uniform(jax.random.fold_in(jax.random.fold_in(own_key, 6), dim), (blocks,), jnp.float32, low / len(shards), top_value / len(shards))
        return jnp.repeat(jnp.exp(draws), dims[dim] // blocks).reshape((-1,) + (1,) * (len(dims) - dim - 1))

    loudness = one(*shards[0])
    for cut in shards[1:]:
        loudness = loudness * one(*cut)
    return loudness


def scatter_about(own_key, extent, width, bound, split=(), kind=jnp.bfloat16):
    values = width * jax.random.normal(own_key, extent, jnp.float32)
    if split:
        values = values * shard_levels(own_key, extent, split, -0.22, 0.18)
    return jnp.clip(values, -bound, bound).astype(kind)


def setup_inputs(seed: int = 0) -> dict:
    seeds = jax.random.split(jax.random.key(seed), 5)
    left_points = draw_left_points(jax.random.fold_in(seeds[4], 71), 0)
    right_points = draw_right_points(jax.random.fold_in(seeds[4], 71), 0)
    left_cotangent = scatter_about(seeds[2], (N, R), 1.0, 6.0, ((0, 512),))
    right_coefficient = scatter_about(seeds[3], (N, R), 1.0, 6.0, ((0, 512),))
    return {"left_points": left_points, "right_points": right_points, "left_cotangent": left_cotangent, "right_coefficient": right_coefficient}


inverse_width = 0.03125
grad_scale = 0.0625
descent_rate = 0.3


def tile_terms(left_bf, left_panel, right_bf, right_panel):
    left_rows = left_bf.shape[0]
    block_rows = min(512, left_rows)
    block_count = left_rows // block_rows
    feature_width = left_bf.shape[1]
    right_wide = right_bf.astype(jnp.float32)
    right_norm = jnp.sum(right_wide * right_wide, axis=1)
    contract_last = (((1,), (1,)), ((), ()))

    def visit_block(carried, pieces):
        accumulated, column_sum = carried
        piece_feat, piece_panel = pieces
        piece_wide = piece_feat.astype(jnp.float32)
        left_norm = jnp.sum(piece_wide * piece_wide, axis=1)
        crossed = lax.dot_general(piece_feat, right_bf, contract_last, preferred_element_type=jnp.float32)
        distance = left_norm[:, None] + right_norm[None, :] - 2.0 * crossed
        kernel = jnp.exp(-inverse_width * distance).astype(jnp.bfloat16)
        weight = lax.dot_general(piece_panel, right_panel, contract_last, preferred_element_type=jnp.float32)
        product = (weight * kernel.astype(jnp.float32)).astype(jnp.bfloat16)
        product_wide = product.astype(jnp.float32)
        left_term = jnp.dot(product, right_bf, preferred_element_type=jnp.float32) - jnp.sum(product_wide, axis=1)[:, None] * piece_wide
        accumulated = accumulated + lax.dot_general(product, piece_feat, (((0,), (0,)), ((), ())), preferred_element_type=jnp.float32)
        column_sum = column_sum + jnp.sum(product_wide, axis=0)
        return (accumulated, column_sum), left_term

    initial = (jnp.zeros((right_bf.shape[0], feature_width), jnp.float32), jnp.zeros((right_bf.shape[0],), jnp.float32))
    pieces = (left_bf.reshape(block_count, block_rows, feature_width), left_panel.reshape(block_count, block_rows, left_panel.shape[1]))
    (accumulated, column_sum), left_terms = lax.scan(visit_block, initial, pieces)
    return left_terms.reshape(left_rows, feature_width), accumulated - column_sum[:, None] * right_wide


def reference(left_points, right_points, left_cotangent, right_coefficient):
    left_values = left_points
    right_values = right_points
    left_grad = jnp.zeros_like(left_points)
    right_grad = jnp.zeros_like(right_points)
    for step_index in range(STEPS):
        left_term, right_term = tile_terms(left_values.astype(jnp.bfloat16), left_cotangent, right_values.astype(jnp.bfloat16), right_coefficient)
        left_grad = left_term * grad_scale
        right_grad = right_term * grad_scale
        left_values = left_values - descent_rate * left_grad
        right_values = right_values - descent_rate * right_grad
    return left_values, right_values, left_grad, right_grad
```

```python
import jax
import jax.numpy as jnp
from jax import lax
from jax.experimental import pallas as pl
from jax.experimental.pallas import tpu as pltpu
from jax.sharding import PartitionSpec as P

STEPS = 2
LOG2E = 1.4426950408889634
PAIR_SCALE = 0.0625 * LOG2E
GRAD_SCALE = 0.0625
RATE = 0.3
MESH = pl.DeviceIdType.MESH
LAST = (((1,), (1,)), ((), ()))

Z_NEAR = (-4, 3, -3, 2, -2, 1, -1)
R_STEP = ((-1, -4), (-1, 4), (1, -4), (1, 4))
X_STEP = (0, 2, 1, 3)


def pair_kernel(lp, rp, lc, rc, lf, rf, lg, rg, lv, rv, gl, gr, own_r, la, lat, ra, rt, prod, kept, lacc, racc,
                ls, lrecv, lhs, lh, rs, rrecv, rhs, rh,
                in_sem, zs, zr, ys, yr, qs, qr, xs, xr, as_, ar, bs, br, cs, cr, ds, dr):
    row, col = lax.axis_index("row"), lax.axis_index("col")
    x, k = row % 4, col % 2
    y = (col // 2) % 4
    z = (col // 8) * 4 + row // 4

    def at(x, y, z, k):
        y, z = (y + 4) % 4, (z + 16) % 16
        return ((z % 4) * 4 + x % 4, (z // 4) * 8 + y * 2 + k)

    side = 2 * k - 1
    relays = (at(x, y, z, 1 - k), at(x, y + side, z, k), at(x, y + side, z, 1 - k))
    sources = (at(x, y, z, 1 - k), at(x, y + 1, z, 0), at(x, y - 1, z, 1))

    barrier = pltpu.get_barrier_semaphore()
    partners = [at(x, y, z + d, k) for d in (-4, -3, -2, -1, 1, 2, 3, 4)]
    partners += [at(x, y, z, 1 - k), at(x, y + side, z, k), at(x, y + side, z, 1 - k), at(x, y - side, z, k)]
    partners += [at(x, y + dy, z + dz, k) for dy, dz in R_STEP]
    partners += [at(x + dx, y, z, k) for dx in (1, 2, 3)]
    for p in partners:
        pl.semaphore_signal(barrier, inc=1, device_id=p, device_id_type=MESH)

    loads = [
        pltpu.make_async_copy(lp, lv, in_sem.at[0]),
        pltpu.make_async_copy(rp, rv, in_sem.at[1]),
        pltpu.make_async_copy(lc, gl.at[2, 0, 4], in_sem.at[2]),
        pltpu.make_async_copy(rc, own_r.at[2], in_sem.at[3]),
    ]
    for c in loads:
        c.start()
    lat[128:144, :] = jnp.ones((16, 2048), jnp.bfloat16)
    for c in loads:
        c.wait()
    gl[0, 0, 4] = lv[...].astype(jnp.bfloat16)
    own_r[0] = rv[...].astype(jnp.bfloat16)
    pl.semaphore_wait(barrier, len(partners))

    def send(src, dst, s, r, device):
        return pltpu.make_async_remote_copy(
            src_ref=src, dst_ref=dst, send_sem=s, recv_sem=r, device_id=device, device_id_type=MESH
        )

    def r_first(ph, s):
        dy, dz = R_STEP[s]
        return send(own_r.at[ph], gr.at[ph, 0, s], qs.at[ph, s], qr.at[ph, s], at(x, y - dy, z - dz, k))

    def l_first(ph, d):
        return send(gl.at[ph, 0, 4], gl.at[ph, 0, d + 4], zs.at[ph, d + 4], zr.at[ph, d + 4], at(x, y, z - d, k))

    def l_second(ph, t):
        c = 1 if t == 0 else 2 + k
        return send(gl.at[ph, 0], gl.at[ph, c], ys.at[ph, t], yr.at[ph, c - 1], relays[t])

    def l_arrived(ph, c):
        return send(gl.at[ph, 0], gl.at[ph, c], ys.at[ph, 0], yr.at[ph, c - 1], relays[0])

    def r_second(ph, i):
        return send(gr.at[ph, 0], gr.at[ph, i], xs.at[ph, i], xr.at[ph, i], at(x + X_STEP[i], y, z, k))

    def gather_start(ph):
        for s in range(4):
            r_first(ph, s).start()
        for d in Z_NEAR:
            l_first(ph, d).start()

    def gather_relay(ph):
        for d in Z_NEAR:
            l_first(ph, d).wait_recv()
        for t in (1, 2, 0):
            l_second(ph, t).start()
        for s in range(4):
            r_first(ph, s).wait_recv()
        for i in (1, 2, 3):
            r_second(ph, i).start()

    def l_back(st, c):
        slot = 0 if c == 1 else 1 + k
        return send(ls.at[st, c - 1], lrecv.at[st, slot], as_.at[st, c - 1], ar.at[st, slot], sources[c - 1])

    def l_back_arrived(st, slot):
        return send(ls.at[st, 0], lrecv.at[st, slot], as_.at[st, 0], ar.at[st, slot], sources[0])

    def l_home(st, d):
        return send(lhs.at[st, d + 4], lh.at[st, d + 4], bs.at[st, d + 4], br.at[st, d + 4], at(x, y, z + d, k))

    def r_back(st, i):
        return send(rs.at[st, i], rrecv.at[st, i], cs.at[st, i], cr.at[st, i], at(x - X_STEP[i], y, z, k))

    def r_home(st, s):
        dy, dz = R_STEP[s]
        return send(rhs.at[st, s], rh.at[st, s], ds.at[st, s], dr.at[st, s], at(x, y + dy, z + dz, k))

    def pieces(v, left):
        norm = jnp.sum(v * v, axis=1, keepdims=True)
        hi = norm.astype(jnp.bfloat16).astype(jnp.float32)
        rest = norm - hi
        mid = rest.astype(jnp.bfloat16).astype(jnp.float32)
        low = rest - mid
        lane = lax.broadcasted_iota(jnp.int32, v.shape, 1)
        if left:
            p, q = (0, 3)
            scale, other = (1.0, 1.0)
        else:
            p, q = (3, 0)
            scale, other = (-0.5, -0.5)
        zero = jnp.zeros_like(v)
        out = jnp.where((lane >= q) & (lane < q + 3), other, zero)
        out = jnp.where(lane == p, scale * hi, out)
        out = jnp.where(lane == p + 1, scale * mid, out)
        return jnp.where(lane == p + 2, scale * low, out).astype(jnp.bfloat16)

    def prepare_left(st, c):
        rows = pl.ds(c * 512, 512)
        a = gl[st, c].reshape(512, 128)
        wide = a.astype(jnp.float32)
        la[rows, :] = pieces(wide, True)
        lat[0:128, rows] = wide.T.astype(jnp.bfloat16)

    def prepare_right(st, i):
        rows = pl.ds(i * 256, 256)
        b = gr[st, i].reshape(256, 128)
        wide = b.astype(jnp.float32)
        ra[rows, :] = pieces(wide, False)
        rt[:, rows] = wide.T

    ones = jnp.ones((512, 128), jnp.bfloat16)

    def produce(st, j, c, slot):
        rows, cols = pl.ds(c * 512, 512), pl.ds(j * 512, 512)
        a = gl[st, c].reshape(512, 128)
        b = gr[st, 2 * j : 2 * j + 2].reshape(512, 128)
        crossed = lax.dot_general(
            jnp.concatenate([a, la[rows, :]], axis=1), jnp.concatenate([b, ra[cols, :]], axis=1),
            LAST, preferred_element_type=jnp.float32,
        )
        if st == 0:
            weight = lax.dot_general(
                gl[2, c].reshape(512, 128), gr[2, 2 * j : 2 * j + 2].reshape(512, 128),
                LAST, preferred_element_type=jnp.float32,
            )
            kept[rows, cols] = weight.astype(jnp.bfloat16)
        else:
            weight = kept[rows, cols].astype(jnp.float32)
        prod[slot] = (weight * jnp.exp2(crossed * PAIR_SCALE)).astype(jnp.bfloat16)

    def consume(st, j, c, slot, first):
        rows = pl.ds(c * 512, 512)
        product = prod[slot]
        b = gr[st, 2 * j : 2 * j + 2].reshape(512, 128)
        left = jnp.dot(product, jnp.concatenate([b, ones], axis=1), preferred_element_type=jnp.float32)
        right = jnp.dot(lat[:, rows], product, preferred_element_type=jnp.float32)
        lacc[rows, :] = left if j == 0 else lacc[rows, :] + left
        racc[j] = right if first else racc[j] + right

    def left_term(st, c):
        rows = pl.ds(c * 512, 512)
        a = gl[st, c].reshape(512, 128).astype(jnp.float32)
        return lacc[rows, 0:128] - lacc[rows, 128:256] * a

    for st in range(STEPS):
        gather_start(st)
        if st == 0:
            gather_start(2)
        gather_relay(st)
        if st == 0:
            gather_relay(2)
        prepare_left(st, 0)
        prepare_right(st, 0)
        for c in (1, 2, 3):
            l_arrived(st, c).wait_recv()
            prepare_left(st, c)
        for i in (1, 2, 3):
            r_second(st, i).wait_recv()
            prepare_right(st, i)
        if st == 0:
            for c in (1, 2, 3):
                l_arrived(2, c).wait_recv()
            for i in (1, 2, 3):
                r_second(2, i).wait_recv()
        tiles = [(j, c) for j in range(2) for c in (2, 3, 1, 0)]
        produce(st, *tiles[0], 0)
        for t, (j, c) in enumerate(tiles):
            consume(st, j, c, t % 2, t % 4 == 0)
            if t < 7:
                produce(st, *tiles[t + 1], (t + 1) % 2)
            if j == 1 and c > 0:
                ls[st, c - 1] = left_term(st, c).astype(jnp.bfloat16)
                l_back(st, c).start()
            if t % 4 == 3:
                for i in (2 * j, 2 * j + 1):
                    cols, half = pl.ds(i * 256, 256), pl.ds((i % 2) * 256, 256)
                    term = racc[j, 0:128, half] - racc[j, 128:129, half] * rt[:, cols]
                    if i == 0:
                        rt[:, cols] = term
                    else:
                        rs[st, i] = term.astype(jnp.bfloat16)
                        r_back(st, i).start()
        for i in (1, 2, 3):
            r_back(st, i).wait_recv()
        total = rt[:, pl.ds(0, 256)]
        for i in (1, 2, 3):
            total = total + rrecv[st, i].astype(jnp.float32)
        rhs[st] = total.T.astype(jnp.bfloat16).reshape(4, 64, 128)
        for s in range(4):
            r_home(st, s).start()
        total = left_term(st, 0)
        for slot in range(3):
            l_back_arrived(st, slot).wait_recv()
            total = total + lrecv[st, slot].astype(jnp.float32)
        lhs[st] = total.astype(jnp.bfloat16).reshape(8, 64, 128)
        for d in Z_NEAR:
            l_home(st, d).start()
        left = lhs[st, 4].astype(jnp.float32)
        for d in Z_NEAR:
            l_home(st, d).wait_recv()
            left = left + lh[st, d + 4].astype(jnp.float32)
        left = left * GRAD_SCALE
        lv[...] = lv[...] - RATE * left
        right = jnp.zeros((64, 128), jnp.float32)
        for s in range(4):
            r_home(st, s).wait_recv()
            right = right + rh[st, s].astype(jnp.float32)
        right = right * GRAD_SCALE
        rv[...] = rv[...] - RATE * right
        if st + 1 < STEPS:
            gl[st + 1, 0, 4] = lv[...].astype(jnp.bfloat16)
            own_r[st + 1] = rv[...].astype(jnp.bfloat16)
        else:
            lf[...] = lv[...]
            rf[...] = rv[...]
            lg[...] = left
            rg[...] = right

    for ph in range(3):
        for d in Z_NEAR:
            l_first(ph, d).wait_send()
        for s in range(4):
            r_first(ph, s).wait_send()
        for t in range(3):
            l_second(ph, t).wait_send()
        for i in (1, 2, 3):
            r_second(ph, i).wait_send()
    for st in range(STEPS):
        for c in (1, 2, 3):
            l_back(st, c).wait_send()
        for d in Z_NEAR:
            l_home(st, d).wait_send()
        for i in (1, 2, 3):
            r_back(st, i).wait_send()
        for s in range(4):
            r_home(st, s).wait_send()


def body(left_points, right_points, left_cotangent, right_coefficient):
    f32, bf16 = jnp.float32, jnp.bfloat16
    dma = pltpu.SemaphoreType.DMA
    block = jax.ShapeDtypeStruct((64, 128), f32)
    return pl.pallas_call(
        pair_kernel,
        name="pairs",
        out_shape=(block,) * 4,
        in_specs=[pl.BlockSpec(memory_space=pl.ANY)] * 4,
        out_specs=[pl.BlockSpec(memory_space=pltpu.VMEM)] * 4,
        scratch_shapes=[
            pltpu.VMEM((64, 128), f32),
            pltpu.VMEM((64, 128), f32),
            pltpu.VMEM((3, 4, 8, 64, 128), bf16),
            pltpu.VMEM((3, 4, 4, 64, 128), bf16),
            pltpu.VMEM((3, 64, 128), bf16),
            pltpu.VMEM((2048, 128), bf16),
            pltpu.VMEM((144, 2048), bf16),
            pltpu.VMEM((1024, 128), bf16),
            pltpu.VMEM((128, 1024), f32),
            pltpu.VMEM((2, 512, 512), bf16),
            pltpu.VMEM((2048, 1024), bf16),
            pltpu.VMEM((2048, 256), f32),
            pltpu.VMEM((2, 144, 512), f32),
            pltpu.VMEM((2, 3, 512, 128), bf16),
            pltpu.VMEM((2, 3, 512, 128), bf16),
            pltpu.VMEM((2, 8, 64, 128), bf16),
            pltpu.VMEM((2, 8, 64, 128), bf16),
            pltpu.VMEM((2, 4, 128, 256), bf16),
            pltpu.VMEM((2, 4, 128, 256), bf16),
            pltpu.VMEM((2, 4, 64, 128), bf16),
            pltpu.VMEM((2, 4, 64, 128), bf16),
            dma((4,)),
            dma((3, 8)), dma((3, 8)),
            dma((3, 3)), dma((3, 3)),
            dma((3, 4)), dma((3, 4)),
            dma((3, 4)), dma((3, 4)),
            dma((2, 3)), dma((2, 3)),
            dma((2, 8)), dma((2, 8)),
            dma((2, 4)), dma((2, 4)),
            dma((2, 4)), dma((2, 4)),
        ],
        compiler_params=pltpu.CompilerParams(
            collective_id=0, has_side_effects=True, vmem_limit_bytes=48 * 2**20
        ),
    )(left_points, right_points, left_cotangent, right_coefficient)


def solution(mesh):
    spec = P(("row", "col"), None)
    return jax.shard_map(body, mesh=mesh, in_specs=(spec,) * 4, out_specs=(spec,) * 4, check_vma=False)
```

```python
import jax
import jax.numpy as jnp
from jax import lax
from jax.experimental import pallas as pl
from jax.experimental.pallas import tpu as pltpu
from jax.sharding import PartitionSpec as P

STEPS = 2
PAIR_SCALE = 0.0625 * 1.4426950408889634
GRAD_SCALE = 0.0625
RATE = 0.3
MESH = pl.DeviceIdType.MESH
LAST = (((1,), (1,)), ((), ()))

Z_LEFT = (-1, 0, 1, 2)
Z_RIGHT = ((-6, 6), (-2, 2))


def pair_kernel(lp, rp, lc, rc, lf, rf, lg, rg, lv, rv, gl, gr, own_r, la, lat, ra, rt, prod, kept, lacc, racc,
                ss, ssr, sx, sxr, sz, szr, ty, tyr, tz, tzr,
                in_sem, lz_s, lz_r, lx_s, lx_r, lk_s, lk_r, rz_s, rz_r, ry_s, ry_r,
                bk_s, bk_r, bx_s, bx_r, bz_s, bz_r, cy_s, cy_r, cz_s, cz_r):
    row, col = lax.axis_index("row"), lax.axis_index("col")
    x, k = row % 4, col % 2
    y = (col // 2) % 4
    z = (col // 8) * 4 + row // 4
    way = 1 - 2 * k

    def at(dx=0, dy=0, dz=0, core=None):
        px, py, pz = (x + dx + 4) % 4, (y + dy + 4) % 4, (z + dz + 16) % 16
        return ((pz % 4) * 4 + px, (pz // 4) * 8 + py * 2 + (k if core is None else core))

    sibling = at(core=1 - k)
    at_x = [None] + [at(dx=i) for i in (1, 2, 3)]
    at_y = [None] + [at(dy=i) for i in (1, 2, 3)]
    z_up = [at(dz=way * o) for o in Z_LEFT]
    z_down = [at(dz=-way * o) for o in Z_LEFT]
    z_far = {o: at(dz=o) for o in (-6, -2, 2, 6)}

    barrier = pltpu.get_barrier_semaphore()
    partners = [z_far[-6], z_far[6], z_far[-2], z_far[2], at(dz=1), at(dz=-1), *at_x[1:], *at_y[1:], sibling]
    for p in partners:
        pl.semaphore_signal(barrier, inc=1, device_id=p, device_id_type=MESH)

    loads = [
        pltpu.make_async_copy(lp, lv, in_sem.at[0]),
        pltpu.make_async_copy(rp, rv, in_sem.at[1]),
        pltpu.make_async_copy(lc, gl.at[2, 0, 0, 1], in_sem.at[2]),
        pltpu.make_async_copy(rc, own_r.at[2], in_sem.at[3]),
    ]
    for c in loads:
        c.start()
    lat[128:144, :] = jnp.ones((16, 2048), jnp.bfloat16)
    for c in loads:
        c.wait()
    gl[0, 0, 0, 1] = lv[...].astype(jnp.bfloat16)
    own_r[0] = rv[...].astype(jnp.bfloat16)
    pl.semaphore_wait(barrier, len(partners))

    def send(src, dst, s, r, device):
        return pltpu.make_async_remote_copy(
            src_ref=src, dst_ref=dst, send_sem=s, recv_sem=r, device_id=device, device_id_type=MESH
        )

    pending = []

    def go(copy):
        copy.start()
        pending.append(copy)

    def l_z(ph, i):
        return send(gl.at[ph, 0, 0, 1], gl.at[ph, 0, 0, i], lz_s.at[ph, i], lz_r.at[ph, i], z_down[i])

    def l_x(ph, i):
        return send(gl.at[ph, 0, 0], gl.at[ph, 0, i], lx_s.at[ph, i], lx_r.at[ph, i], at_x[i])

    def l_k(ph, i):
        return send(gl.at[ph, 0, i], gl.at[ph, 1, i], lk_s.at[ph, i], lk_r.at[ph, i], sibling)

    def r_z(ph, h, s):
        n = 2 * h + s
        return send(own_r.at[ph], gr.at[ph, h, 0, s], rz_s.at[ph, n], rz_r.at[ph, n], z_far[-Z_RIGHT[h][s]])

    def r_y(ph, h, i):
        n = 4 * h + i
        return send(gr.at[ph, h, 0], gr.at[ph, h, i], ry_s.at[ph, n], ry_r.at[ph, n], at_y[i])

    def gather_start(ph):
        go(r_z(ph, 0, 0))
        go(r_z(ph, 0, 1))
        for i in (3, 0, 2):
            go(l_z(ph, i))
        go(r_z(ph, 1, 0))
        go(r_z(ph, 1, 1))

    def relay_left(ph):
        for i in (0, 2, 3):
            l_z(ph, i).wait_recv()
        for i in (2, 1, 3):
            go(l_x(ph, i))
        go(l_k(ph, 0))

    def relay_right(ph, h):
        r_z(ph, h, 0).wait_recv()
        r_z(ph, h, 1).wait_recv()
        for i in (2, 1, 3):
            go(r_y(ph, h, i))

    def relay_sibling(ph):
        for i in (1, 3, 2):
            l_x(ph, i).wait_recv()
            go(l_k(ph, i))

    def b_k(st, c):
        return send(ss.at[st, c], ssr.at[st, c], bk_s.at[st, c], bk_r.at[st, c], sibling)

    def b_x(st, i):
        return send(sx.at[st, i], sxr.at[st, i], bx_s.at[st, i], bx_r.at[st, i], at_x[4 - i])

    def b_z(st, i):
        return send(sz.at[st, i], szr.at[st, i], bz_s.at[st, i], bz_r.at[st, i], z_up[i])

    def c_y(st, h, i):
        n = 4 * h + i
        return send(ty.at[st, h, i], tyr.at[st, h, i], cy_s.at[st, n], cy_r.at[st, n], at_y[4 - i])

    def c_z(st, h, s):
        n = 2 * h + s
        return send(tz.at[st, n], tzr.at[st, n], cz_s.at[st, n], cz_r.at[st, n], z_far[Z_RIGHT[h][s]])

    def pieces(v, own, other, scale):
        norm = jnp.sum(v * v, axis=1, keepdims=True)
        hi = norm.astype(jnp.bfloat16).astype(jnp.float32)
        rest = norm - hi
        mid = rest.astype(jnp.bfloat16).astype(jnp.float32)
        low = rest - mid
        lane = lax.broadcasted_iota(jnp.int32, v.shape, 1)
        out = jnp.where((lane >= other) & (lane < other + 3), scale, jnp.zeros_like(v))
        out = jnp.where(lane == own, scale * hi, out)
        out = jnp.where(lane == own + 1, scale * mid, out)
        return jnp.where(lane == own + 2, scale * low, out).astype(jnp.bfloat16)

    def prepare_left(st, m, i):
        rows = pl.ds((4 * m + i) * 256, 256)
        wide = gl[st, m, i].reshape(256, 128).astype(jnp.float32)
        la[rows, :] = pieces(wide, 0, 3, 1.0)
        lat[0:128, rows] = wide.T.astype(jnp.bfloat16)

    def prepare_right(st, h, i):
        rows = pl.ds((4 * h + i) * 128, 128)
        wide = gr[st, h, i].reshape(128, 128).astype(jnp.float32)
        ra[rows, :] = pieces(wide, 3, 0, -0.5)
        rt[:, rows] = wide.T

    ones = jnp.ones((512, 128), jnp.bfloat16)

    def lefts(ph, c):
        return gl[ph, c // 2, 2 * (c % 2) : 2 * (c % 2) + 2].reshape(512, 128)

    def produce(st, h, c, slot):
        rows, cols = pl.ds(c * 512, 512), pl.ds(h * 512, 512)
        crossed = lax.dot_general(
            jnp.concatenate([lefts(st, c), la[rows, :]], axis=1),
            jnp.concatenate([gr[st, h].reshape(512, 128), ra[cols, :]], axis=1),
            LAST, preferred_element_type=jnp.float32,
        )
        if st == 0:
            weight = lax.dot_general(
                lefts(2, c), gr[2, h].reshape(512, 128), LAST, preferred_element_type=jnp.float32
            )
            kept[rows, cols] = weight.astype(jnp.bfloat16)
        else:
            weight = kept[rows, cols].astype(jnp.float32)
        prod[slot] = (weight * jnp.exp2(crossed * PAIR_SCALE)).astype(jnp.bfloat16)

    def consume(st, h, c, slot, first_h, first_c):
        rows = pl.ds(c * 512, 512)
        product = prod[slot]
        b = gr[st, h].reshape(512, 128)
        left = jnp.dot(product, jnp.concatenate([b, ones], axis=1), preferred_element_type=jnp.float32)
        right = jnp.dot(lat[:, rows], product, preferred_element_type=jnp.float32)
        lacc[rows, :] = left if first_h else lacc[rows, :] + left
        racc[h] = right if first_c else racc[h] + right

    def left_term(st, c):
        rows = pl.ds(c * 512, 512)
        return lacc[rows, 0:128] - lacc[rows, 128:256] * lefts(st, c).astype(jnp.float32)

    def right_out(st, h):
        term = racc[h, 0:128, :] - racc[h, 128:129, :] * rt[:, pl.ds(h * 512, 512)]
        rt[:, pl.ds(h * 512, 128)] = term[:, 0:128]
        for i in (2, 1, 3):
            ty[st, h, i] = term[:, 128 * i : 128 * i + 128].astype(jnp.bfloat16)
            go(c_y(st, h, i))

    def right_home(st, h):
        total = rt[:, pl.ds(h * 512, 128)]
        for i in (1, 3, 2):
            c_y(st, h, i).wait_recv()
            total = total + tyr[st, h, i].astype(jnp.float32)
        tz[st, 2 * h : 2 * h + 2] = total.T.astype(jnp.bfloat16).reshape(2, 64, 128)
        go(c_z(st, h, 0))
        go(c_z(st, h, 1))

    for st in range(STEPS):
        gather_start(st)
        if st == 0:
            gather_start(2)
        relay_left(st)
        relay_right(st, 1)
        prepare_left(st, 0, 0)
        relay_right(st, 0)
        if st == 0:
            relay_left(2)
            relay_right(2, 1)
            relay_right(2, 0)
        relay_sibling(st)
        for i in (1, 2, 3):
            prepare_left(st, 0, i)
        for h in (1, 0):
            for i in range(4):
                if i:
                    r_y(st, h, i).wait_recv()
                prepare_right(st, h, i)
        if st == 0:
            relay_sibling(2)
        for i in range(4):
            l_k(st, i).wait_recv()
            prepare_left(st, 1, i)
        if st == 0:
            for h in range(2):
                for i in (1, 2, 3):
                    r_y(2, h, i).wait_recv()
            for i in range(4):
                l_k(2, i).wait_recv()

        tiles = [(0, c) for c in (0, 1, 2, 3)] + [(1, c) for c in (3, 2, 1, 0)]
        produce(st, *tiles[0], 0)
        for t, (h, c) in enumerate(tiles):
            consume(st, h, c, t % 2, h == 0, t % 4 == 0)
            if t < 7:
                produce(st, *tiles[t + 1], (t + 1) % 2)
            if t == 3:
                right_out(st, 0)
            if h == 1 and c >= 2:
                ss[st, c - 2] = left_term(st, c).astype(jnp.bfloat16)
                go(b_k(st, c - 2))
            if h == 1 and c == 1:
                b_k(st, 1).wait_recv()
                total = left_term(st, 1) + ssr[st, 1].astype(jnp.float32)
                sx[st, 2:4] = total.astype(jnp.bfloat16).reshape(2, 256, 128)
                go(b_x(st, 2))
                go(b_x(st, 3))
        b_k(st, 0).wait_recv()
        total = left_term(st, 0) + ssr[st, 0].astype(jnp.float32)
        sx[st, 1] = total[256:512].astype(jnp.bfloat16)
        go(b_x(st, 1))
        right_out(st, 1)
        right_home(st, 0)
        total = total[0:256]
        for i in (3, 2, 1):
            b_x(st, i).wait_recv()
            total = total + sxr[st, i].astype(jnp.float32)
        sz[st] = total.astype(jnp.bfloat16).reshape(4, 64, 128)
        for i in (3, 0, 2):
            go(b_z(st, i))
        left = total[64:128]
        right_home(st, 1)
        for i in (0, 2, 3):
            b_z(st, i).wait_recv()
            left = left + szr[st, i].astype(jnp.float32)
        left = left * GRAD_SCALE
        lv[...] = lv[...] - RATE * left
        if st + 1 < STEPS:
            gl[st + 1, 0, 0, 1] = lv[...].astype(jnp.bfloat16)
        right = jnp.zeros((64, 128), jnp.float32)
        for h in (1, 0):
            for s in range(2):
                c_z(st, h, s).wait_recv()
                right = right + tzr[st, 2 * h + s].astype(jnp.float32)
        right = right * GRAD_SCALE
        rv[...] = rv[...] - RATE * right
        if st + 1 < STEPS:
            own_r[st + 1] = rv[...].astype(jnp.bfloat16)
        else:
            lf[...] = lv[...]
            rf[...] = rv[...]
            lg[...] = left
            rg[...] = right

    for copy in pending:
        copy.wait_send()


def body(left_points, right_points, left_cotangent, right_coefficient):
    f32, bf16 = jnp.float32, jnp.bfloat16
    dma = pltpu.SemaphoreType.DMA
    block = jax.ShapeDtypeStruct((64, 128), f32)
    return pl.pallas_call(
        pair_kernel,
        name="pairs",
        out_shape=(block,) * 4,
        in_specs=[pl.BlockSpec(memory_space=pl.ANY)] * 4,
        out_specs=[pl.BlockSpec(memory_space=pltpu.VMEM)] * 4,
        scratch_shapes=[
            pltpu.VMEM((64, 128), f32),
            pltpu.VMEM((64, 128), f32),
            pltpu.VMEM((3, 2, 4, 4, 64, 128), bf16),
            pltpu.VMEM((3, 2, 4, 2, 64, 128), bf16),
            pltpu.VMEM((3, 64, 128), bf16),
            pltpu.VMEM((2048, 128), bf16),
            pltpu.VMEM((144, 2048), bf16),
            pltpu.VMEM((1024, 128), bf16),
            pltpu.VMEM((128, 1024), f32),
            pltpu.VMEM((2, 512, 512), bf16),
            pltpu.VMEM((2048, 1024), bf16),
            pltpu.VMEM((2048, 256), f32),
            pltpu.VMEM((2, 144, 512), f32),
            pltpu.VMEM((2, 2, 512, 128), bf16),
            pltpu.VMEM((2, 2, 512, 128), bf16),
            pltpu.VMEM((2, 4, 256, 128), bf16),
            pltpu.VMEM((2, 4, 256, 128), bf16),
            pltpu.VMEM((2, 4, 64, 128), bf16),
            pltpu.VMEM((2, 4, 64, 128), bf16),
            pltpu.VMEM((2, 2, 4, 128, 128), bf16),
            pltpu.VMEM((2, 2, 4, 128, 128), bf16),
            pltpu.VMEM((2, 4, 64, 128), bf16),
            pltpu.VMEM((2, 4, 64, 128), bf16),
            dma((4,)),
            dma((3, 4)), dma((3, 4)),
            dma((3, 4)), dma((3, 4)),
            dma((3, 4)), dma((3, 4)),
            dma((3, 4)), dma((3, 4)),
            dma((3, 8)), dma((3, 8)),
            dma((2, 2)), dma((2, 2)),
            dma((2, 4)), dma((2, 4)),
            dma((2, 4)), dma((2, 4)),
            dma((2, 8)), dma((2, 8)),
            dma((2, 4)), dma((2, 4)),
        ],
        compiler_params=pltpu.CompilerParams(
            collective_id=0, has_side_effects=True, vmem_limit_bytes=64 * 2**20 - 2**16
        ),
    )(left_points, right_points, left_cotangent, right_coefficient)


def solution(mesh):
    spec = P(("row", "col"), None)
    return jax.shard_map(body, mesh=mesh, in_specs=(spec,) * 4, out_specs=(spec,) * 4, check_vma=False)
```

```python
import jax
import jax.numpy as jnp
from jax import lax
from jax.experimental import pallas as pl
from jax.experimental.pallas import tpu as pltpu
from jax.sharding import PartitionSpec as P

STEPS = 2
PAIR_SCALE = 0.0625 * 1.4426950408889634
GRAD_SCALE = 0.0625
RATE = 0.3
MESH = pl.DeviceIdType.MESH
LAST = (((1,), (1,)), ((), ()))

Z_LEFT = (-1, 0, 1, 2)
Z_RIGHT = ((-6, 6), (-2, 2))


def pair_kernel(lp, rp, lc, rc, result, lv, rv, gl, gr, own_r, la, lat, ra, rt, prod, kept, lacc, racc,
                ss, ssr, sx, sxr, sz, szr, ty, tyr, tz, tzr,
                in_sem, lz_s, lz_r, lx_s, lx_r, lk_s, lk_r, rz_s, rz_r, ry_s, ry_r,
                bk_s, bk_r, bx_s, bx_r, bz_s, bz_r, cy_s, cy_r, cz_s, cz_r):
    row, col = lax.axis_index("row"), lax.axis_index("col")
    x, k = row % 4, col % 2
    y = (col // 2) % 4
    z = (col // 8) * 4 + row // 4
    way = 1 - 2 * k

    def at(dx=0, dy=0, dz=0, core=None):
        px, py, pz = (x + dx + 4) % 4, (y + dy + 4) % 4, (z + dz + 16) % 16
        return ((pz % 4) * 4 + px, (pz // 4) * 8 + py * 2 + (k if core is None else core))

    sibling = at(core=1 - k)
    at_x = [None] + [at(dx=i) for i in (1, 2, 3)]
    at_y = [None] + [at(dy=i) for i in (1, 2, 3)]
    z_up = [at(dz=way * o) for o in Z_LEFT]
    z_down = [at(dz=-way * o) for o in Z_LEFT]
    z_far = {o: at(dz=o) for o in (-6, -2, 2, 6)}

    barrier = pltpu.get_barrier_semaphore()
    partners = [z_far[-6], z_far[6], z_far[-2], z_far[2], at(dz=1), at(dz=-1), *at_x[1:], *at_y[1:], sibling]
    for p in partners:
        pl.semaphore_signal(barrier, inc=1, device_id=p, device_id_type=MESH)

    loads = [
        pltpu.make_async_copy(lp, lv, in_sem.at[0]),
        pltpu.make_async_copy(rp, rv, in_sem.at[1]),
        pltpu.make_async_copy(lc, gl.at[2, 0, 0, 1], in_sem.at[2]),
        pltpu.make_async_copy(rc, own_r.at[2], in_sem.at[3]),
    ]
    for c in loads:
        c.start()
    lat[128:144, :] = jnp.ones((16, 2048), jnp.bfloat16)
    for c in loads:
        c.wait()
    gl[0, 0, 0, 1] = lv[...].astype(jnp.bfloat16)
    own_r[0] = rv[...].astype(jnp.bfloat16)
    pl.semaphore_wait(barrier, len(partners))

    def send(src, dst, s, r, device):
        return pltpu.make_async_remote_copy(
            src_ref=src, dst_ref=dst, send_sem=s, recv_sem=r, device_id=device, device_id_type=MESH
        )

    pending = []

    def go(copy):
        copy.start()
        pending.append(copy)

    def sent(keep):
        for copy in pending[: len(pending) - keep]:
            copy.wait_send()
        del pending[: len(pending) - keep]

    def l_z(ph, i):
        return send(gl.at[ph, 0, 0, 1], gl.at[ph, 0, 0, i], lz_s.at[ph, i], lz_r.at[ph, i], z_down[i])

    def l_x(ph, i):
        return send(gl.at[ph, 0, 0], gl.at[ph, 0, i], lx_s.at[ph, i], lx_r.at[ph, i], at_x[i])

    def l_k(ph, i):
        return send(gl.at[ph, 0, i], gl.at[ph, 1, i], lk_s.at[ph, i], lk_r.at[ph, i], sibling)

    def r_z(ph, h, s):
        n = 2 * h + s
        return send(own_r.at[ph], gr.at[ph, h, 0, s], rz_s.at[ph, n], rz_r.at[ph, n], z_far[-Z_RIGHT[h][s]])

    def r_y(ph, h, i):
        n = 4 * h + i
        return send(gr.at[ph, h, 0], gr.at[ph, h, i], ry_s.at[ph, n], ry_r.at[ph, n], at_y[i])

    def gather_start(ph):
        go(r_z(ph, 0, 0))
        go(r_z(ph, 0, 1))
        for i in (3, 0, 2):
            go(l_z(ph, i))
        go(r_z(ph, 1, 0))
        go(r_z(ph, 1, 1))

    def relay_left(ph):
        for i in (0, 2, 3):
            l_z(ph, i).wait_recv()
        for i in (2, 1, 3):
            go(l_x(ph, i))
        go(l_k(ph, 0))

    def relay_right(ph, h):
        r_z(ph, h, 0).wait_recv()
        r_z(ph, h, 1).wait_recv()
        for i in (2, 1, 3):
            go(r_y(ph, h, i))

    def relay_sibling(ph):
        for i in (1, 3, 2):
            l_x(ph, i).wait_recv()
            go(l_k(ph, i))

    def b_k(st, c):
        return send(ss.at[st, c], ssr.at[st, c], bk_s.at[st, c], bk_r.at[st, c], sibling)

    def b_x(st, i):
        return send(sx.at[st, i], sxr.at[st, i], bx_s.at[st, i], bx_r.at[st, i], at_x[4 - i])

    def b_z(st, i):
        return send(sz.at[st, i], szr.at[st, i], bz_s.at[st, i], bz_r.at[st, i], z_up[i])

    def c_y(st, h, i):
        n = 4 * h + i
        return send(ty.at[st, h, i], tyr.at[st, h, i], cy_s.at[st, n], cy_r.at[st, n], at_y[4 - i])

    def c_z(st, h, s):
        n = 2 * h + s
        return send(tz.at[st, n], tzr.at[st, n], cz_s.at[st, n], cz_r.at[st, n], z_far[Z_RIGHT[h][s]])

    def pieces(v, own, other, scale):
        norm = jnp.sum(v * v, axis=1, keepdims=True)
        hi = norm.astype(jnp.bfloat16).astype(jnp.float32)
        rest = norm - hi
        mid = rest.astype(jnp.bfloat16).astype(jnp.float32)
        low = rest - mid
        lane = lax.broadcasted_iota(jnp.int32, v.shape, 1)
        out = jnp.where((lane >= other) & (lane < other + 3), scale, jnp.zeros_like(v))
        out = jnp.where(lane == own, scale * hi, out)
        out = jnp.where(lane == own + 1, scale * mid, out)
        return jnp.where(lane == own + 2, scale * low, out).astype(jnp.bfloat16)

    def prepare_left(st, m, i):
        rows = pl.ds((4 * m + i) * 256, 256)
        wide = gl[st, m, i].reshape(256, 128).astype(jnp.float32)
        la[rows, :] = pieces(wide, 0, 3, 1.0)
        lat[0:128, rows] = wide.T.astype(jnp.bfloat16)

    def prepare_right(st, h, i):
        rows = pl.ds((4 * h + i) * 128, 128)
        wide = gr[st, h, i].reshape(128, 128).astype(jnp.float32)
        ra[rows, :] = pieces(wide, 3, 0, -0.5)
        rt[:, rows] = wide.T

    ones = jnp.ones((512, 128), jnp.bfloat16)

    def lefts(ph, c):
        return gl[ph, c // 2, 2 * (c % 2) : 2 * (c % 2) + 2].reshape(512, 128)

    def factor(st, h, c):
        rows, cols = pl.ds(c * 512, 512), pl.ds(h * 512, 512)
        crossed = lax.dot_general(
            jnp.concatenate([lefts(st, c), la[rows, :]], axis=1),
            jnp.concatenate([gr[st, h].reshape(512, 128), ra[cols, :]], axis=1),
            LAST, preferred_element_type=jnp.float32,
        )
        return jnp.exp2(crossed * PAIR_SCALE)

    def produce(st, h, c, slot):
        rows, cols = pl.ds(c * 512, 512), pl.ds(h * 512, 512)
        if st == 0:
            weight = lax.dot_general(
                lefts(2, c), gr[2, h].reshape(512, 128), LAST, preferred_element_type=jnp.float32
            )
            prod[slot] = (weight * kept[rows, cols].astype(jnp.float32)).astype(jnp.bfloat16)
            kept[rows, cols] = weight.astype(jnp.bfloat16)
        else:
            prod[slot] = (kept[rows, cols].astype(jnp.float32) * factor(st, h, c)).astype(jnp.bfloat16)

    def consume(st, h, c, slot, first_h, first_c):
        rows = pl.ds(c * 512, 512)
        product = prod[slot]
        b = gr[st, h].reshape(512, 128)
        left = jnp.dot(product, jnp.concatenate([b, ones], axis=1), preferred_element_type=jnp.float32)
        right = jnp.dot(lat[:, rows], product, preferred_element_type=jnp.float32)
        lacc[rows, :] = left if first_h else lacc[rows, :] + left
        racc[h] = right if first_c else racc[h] + right

    def left_term(st, c):
        rows = pl.ds(c * 512, 512)
        return lacc[rows, 0:128] - lacc[rows, 128:256] * lefts(st, c).astype(jnp.float32)

    def right_out(st, h):
        term = racc[h, 0:128, :] - racc[h, 128:129, :] * rt[:, pl.ds(h * 512, 512)]
        rt[:, pl.ds(h * 512, 128)] = term[:, 0:128]
        for i in (2, 1, 3):
            ty[st, h, i] = term[:, 128 * i : 128 * i + 128].astype(jnp.bfloat16)
            go(c_y(st, h, i))

    def right_home(st, h):
        total = rt[:, pl.ds(h * 512, 128)]
        for i in (1, 3, 2):
            c_y(st, h, i).wait_recv()
            total = total + tyr[st, h, i].astype(jnp.float32)
        tz[st, 2 * h : 2 * h + 2] = total.T.astype(jnp.bfloat16).reshape(2, 64, 128)
        go(c_z(st, h, 0))
        go(c_z(st, h, 1))

    for st in range(STEPS):
        gather_start(st)
        if st == 0:
            gather_start(2)
        else:
            sent(7)
        relay_left(st)
        relay_right(st, 1)
        prepare_left(st, 0, 0)
        relay_right(st, 0)
        if st == 0:
            relay_left(2)
            relay_right(2, 1)
            relay_right(2, 0)
        relay_sibling(st)
        for i in (1, 2, 3):
            prepare_left(st, 0, i)
        for h in (1, 0):
            for i in range(4):
                if i:
                    r_y(st, h, i).wait_recv()
                prepare_right(st, h, i)
        if st == 0:
            relay_sibling(2)
        for i in range(4):
            l_k(st, i).wait_recv()
            prepare_left(st, 1, i)
        if st == 0:
            for h in range(2):
                for c in range(4):
                    kept[pl.ds(c * 512, 512), pl.ds(h * 512, 512)] = factor(0, h, c).astype(jnp.bfloat16)
            for h in range(2):
                for i in (1, 2, 3):
                    r_y(2, h, i).wait_recv()
            for i in range(4):
                l_k(2, i).wait_recv()

        tiles = [(0, c) for c in (0, 1, 2, 3)] + [(1, c) for c in (3, 2, 1, 0)]
        produce(st, *tiles[0], 0)
        for t, (h, c) in enumerate(tiles):
            consume(st, h, c, t % 2, h == 0, t % 4 == 0)
            if t < 7:
                produce(st, *tiles[t + 1], (t + 1) % 2)
            if t == 3:
                right_out(st, 0)
            if h == 1 and c >= 2:
                ss[st, c - 2] = left_term(st, c).astype(jnp.bfloat16)
                go(b_k(st, c - 2))
            if h == 1 and c == 1:
                b_k(st, 1).wait_recv()
                total = left_term(st, 1) + ssr[st, 1].astype(jnp.float32)
                sx[st, 2:4] = total.astype(jnp.bfloat16).reshape(2, 256, 128)
                go(b_x(st, 2))
                go(b_x(st, 3))
        b_k(st, 0).wait_recv()
        total = left_term(st, 0) + ssr[st, 0].astype(jnp.float32)
        sx[st, 1] = total[256:512].astype(jnp.bfloat16)
        go(b_x(st, 1))
        right_out(st, 1)
        right_home(st, 0)
        total = total[0:256]
        for i in (3, 2, 1):
            b_x(st, i).wait_recv()
            total = total + sxr[st, i].astype(jnp.float32)
        sz[st] = total.astype(jnp.bfloat16).reshape(4, 64, 128)
        for i in (3, 0, 2):
            go(b_z(st, i))
        left = total[64:128]
        right_home(st, 1)
        if st + 1 == STEPS:
            sent(5)
        for i in (0, 2, 3):
            b_z(st, i).wait_recv()
            left = left + szr[st, i].astype(jnp.float32)
        if st + 1 < STEPS:
            lv[...] = lv[...] - RATE * (left * GRAD_SCALE)
            gl[st + 1, 0, 0, 1] = lv[...].astype(jnp.bfloat16)
        right = jnp.zeros((64, 128), jnp.float32)
        for h in (1, 0):
            for s in range(2):
                c_z(st, h, s).wait_recv()
                right = right + tzr[st, 2 * h + s].astype(jnp.float32)
        if st + 1 < STEPS:
            rv[...] = rv[...] - RATE * (right * GRAD_SCALE)
            own_r[st + 1] = rv[...].astype(jnp.bfloat16)
        else:
            left, right = left * GRAD_SCALE, right * GRAD_SCALE
            result[0:64, :] = lv[...] - RATE * left
            result[64:128, :] = rv[...] - RATE * right
            result[128:192, :] = left
            result[192:256, :] = right

    sent(0)


def body(left_points, right_points, left_cotangent, right_coefficient):
    f32, bf16 = jnp.float32, jnp.bfloat16
    dma = pltpu.SemaphoreType.DMA
    result = pl.pallas_call(
        pair_kernel,
        name="pairs",
        out_shape=jax.ShapeDtypeStruct((256, 128), f32),
        in_specs=[pl.BlockSpec(memory_space=pl.ANY)] * 4,
        out_specs=pl.BlockSpec(memory_space=pltpu.VMEM),
        scratch_shapes=[
            pltpu.VMEM((64, 128), f32),
            pltpu.VMEM((64, 128), f32),
            pltpu.VMEM((3, 2, 4, 4, 64, 128), bf16),
            pltpu.VMEM((3, 2, 4, 2, 64, 128), bf16),
            pltpu.VMEM((3, 64, 128), bf16),
            pltpu.VMEM((2048, 128), bf16),
            pltpu.VMEM((144, 2048), bf16),
            pltpu.VMEM((1024, 128), bf16),
            pltpu.VMEM((128, 1024), f32),
            pltpu.VMEM((2, 512, 512), bf16),
            pltpu.VMEM((2048, 1024), bf16),
            pltpu.VMEM((2048, 256), f32),
            pltpu.VMEM((2, 144, 512), f32),
            pltpu.VMEM((2, 2, 512, 128), bf16),
            pltpu.VMEM((2, 2, 512, 128), bf16),
            pltpu.VMEM((2, 4, 256, 128), bf16),
            pltpu.VMEM((2, 4, 256, 128), bf16),
            pltpu.VMEM((2, 4, 64, 128), bf16),
            pltpu.VMEM((2, 4, 64, 128), bf16),
            pltpu.VMEM((2, 2, 4, 128, 128), bf16),
            pltpu.VMEM((2, 2, 4, 128, 128), bf16),
            pltpu.VMEM((2, 4, 64, 128), bf16),
            pltpu.VMEM((2, 4, 64, 128), bf16),
            dma((4,)),
            dma((3, 4)), dma((3, 4)),
            dma((3, 4)), dma((3, 4)),
            dma((3, 4)), dma((3, 4)),
            dma((3, 4)), dma((3, 4)),
            dma((3, 8)), dma((3, 8)),
            dma((2, 2)), dma((2, 2)),
            dma((2, 4)), dma((2, 4)),
            dma((2, 4)), dma((2, 4)),
            dma((2, 8)), dma((2, 8)),
            dma((2, 4)), dma((2, 4)),
        ],
        compiler_params=pltpu.CompilerParams(
            collective_id=0, has_side_effects=True, vmem_limit_bytes=64 * 2**20 - 2**16
        ),
    )(left_points, right_points, left_cotangent, right_coefficient)
    return tuple(result[64 * i : 64 * i + 64] for i in range(4))


def solution(mesh):
    spec = P(("row", "col"), None)
    return jax.shard_map(body, mesh=mesh, in_specs=(spec,) * 4, out_specs=(spec,) * 4, check_vma=False)
```

```python
import jax
import jax.numpy as jnp
from jax import lax
from jax.experimental import pallas as pl
from jax.experimental.pallas import tpu as pltpu
from jax.sharding import PartitionSpec as P

STEPS = 2
PAIR_SCALE = 0.0625 * 1.4426950408889634
GRAD_SCALE = 0.0625
RATE = 0.3
MESH = pl.DeviceIdType.MESH
LAST = (((1,), (1,)), ((), ()))

Z_LEFT = (-3, -1, 1, 3)
Z_RIGHT = ((5, -4), (-3, 4))


def pair_kernel(lp, rp, lc, rc, result, lv, rv, gl, gr, own_l, own_r, la, lat, ra, rt, prod, kept, lacc, racc,
                ss, ssr, sx, sxr, sz, szr, ty, tyr, tz, tzr,
                in_sem, lz_s, lz_r, lx_s, lx_r, lk_s, lk_r, rz_s, rz_r, ry_s, ry_r,
                bk_s, bk_r, bx_s, bx_r, bz_s, bz_r, cy_s, cy_r, cz_s, cz_r):
    row, col = lax.axis_index("row"), lax.axis_index("col")
    x, k = row % 4, col % 2
    y = (col // 2) % 4
    z = (col // 8) * 4 + row // 4
    way = 1 - 2 * k

    def at(dx=0, dy=0, dz=0, core=None):
        px, py, pz = (x + dx + 4) % 4, (y + dy + 4) % 4, (z + dz + 16) % 16
        return ((pz % 4) * 4 + px, (pz // 4) * 8 + py * 2 + (k if core is None else core))

    sibling = at(core=1 - k)
    at_x = [None] + [at(dx=i) for i in (1, 2, 3)]
    at_y = [None] + [at(dy=i) for i in (1, 2, 3)]
    z_left = {o: at(dz=o) for o in Z_LEFT}
    z_right = {o: at(dz=way * o) for o in (-5, -4, -3, 3, 4, 5)}

    barrier = pltpu.get_barrier_semaphore()
    partners = [*z_left.values(), z_right[-4], z_right[4], z_right[-5], z_right[5], *at_x[1:], *at_y[1:], sibling]
    for p in partners:
        pl.semaphore_signal(barrier, inc=1, device_id=p, device_id_type=MESH)

    loads = [
        pltpu.make_async_copy(lp, lv, in_sem.at[0]),
        pltpu.make_async_copy(rp, rv, in_sem.at[1]),
        pltpu.make_async_copy(lc, own_l.at[2], in_sem.at[2]),
        pltpu.make_async_copy(rc, own_r.at[2], in_sem.at[3]),
    ]
    for c in loads:
        c.start()
    lat[128:144, :] = jnp.ones((16, 2048), jnp.bfloat16)
    for c in loads:
        c.wait()
    own_l[0] = lv[...].astype(jnp.bfloat16)
    own_r[0] = rv[...].astype(jnp.bfloat16)
    pl.semaphore_wait(barrier, len(partners))

    def send(src, dst, s, r, device):
        return pltpu.make_async_remote_copy(
            src_ref=src, dst_ref=dst, send_sem=s, recv_sem=r, device_id=device, device_id_type=MESH
        )

    pending = []

    def go(copy):
        copy.start()
        pending.append(copy)

    def sent(keep):
        for copy in pending[: len(pending) - keep]:
            copy.wait_send()
        del pending[: len(pending) - keep]

    def l_z(ph, i):
        return send(own_l.at[ph], gl.at[ph, 0, 0, i], lz_s.at[ph, i], lz_r.at[ph, i], z_left[-Z_LEFT[i]])

    def l_x(ph, i):
        return send(gl.at[ph, 0, 0], gl.at[ph, 0, i], lx_s.at[ph, i], lx_r.at[ph, i], at_x[i])

    def l_k(ph, i):
        return send(gl.at[ph, 0, i], gl.at[ph, 1, i], lk_s.at[ph, i], lk_r.at[ph, i], sibling)

    def r_z(ph, h, s):
        n = 2 * h + s
        return send(own_r.at[ph], gr.at[ph, h, 0, s], rz_s.at[ph, n], rz_r.at[ph, n], z_right[-Z_RIGHT[h][s]])

    def r_y(ph, h, i):
        n = 4 * h + i
        return send(gr.at[ph, h, 0], gr.at[ph, h, i], ry_s.at[ph, n], ry_r.at[ph, n], at_y[i])

    def start_left(ph):
        for i in (0, 3, 1, 2):
            go(l_z(ph, i))

    def start_right(ph, h):
        go(r_z(ph, h, 0))
        go(r_z(ph, h, 1))

    def relay_left(ph):
        for i in (1, 2, 0, 3):
            l_z(ph, i).wait_recv()
        for i in (2, 1, 3):
            go(l_x(ph, i))
        go(l_k(ph, 0))

    def relay_right(ph, h):
        r_z(ph, h, 0).wait_recv()
        r_z(ph, h, 1).wait_recv()
        for i in (2, 1, 3):
            go(r_y(ph, h, i))

    def relay_sibling(ph):
        for i in (1, 3, 2):
            l_x(ph, i).wait_recv()
            go(l_k(ph, i))

    def b_k(st, c):
        return send(ss.at[st, c], ssr.at[st, c], bk_s.at[st, c], bk_r.at[st, c], sibling)

    def b_x(st, i):
        return send(sx.at[st, i], sxr.at[st, i], bx_s.at[st, i], bx_r.at[st, i], at_x[4 - i])

    def b_z(st, i):
        return send(sz.at[st, i], szr.at[st, i], bz_s.at[st, i], bz_r.at[st, i], z_left[Z_LEFT[i]])

    def c_y(st, h, i):
        n = 4 * h + i
        return send(ty.at[st, h, i], tyr.at[st, h, i], cy_s.at[st, n], cy_r.at[st, n], at_y[4 - i])

    def c_z(st, h, s):
        n = 2 * h + s
        return send(tz.at[st, n], tzr.at[st, n], cz_s.at[st, n], cz_r.at[st, n], z_right[Z_RIGHT[h][s]])

    def pieces(v, own, other, scale):
        norm = jnp.sum(v * v, axis=1, keepdims=True)
        hi = norm.astype(jnp.bfloat16).astype(jnp.float32)
        rest = norm - hi
        mid = rest.astype(jnp.bfloat16).astype(jnp.float32)
        low = rest - mid
        lane = lax.broadcasted_iota(jnp.int32, v.shape, 1)
        out = jnp.where((lane >= other) & (lane < other + 3), scale, jnp.zeros_like(v))
        out = jnp.where(lane == own, scale * hi, out)
        out = jnp.where(lane == own + 1, scale * mid, out)
        return jnp.where(lane == own + 2, scale * low, out).astype(jnp.bfloat16)

    def prepare_left(st, m, i):
        rows = pl.ds((4 * m + i) * 256, 256)
        wide = gl[st, m, i].reshape(256, 128).astype(jnp.float32)
        la[rows, :] = pieces(wide, 0, 3, 1.0)
        lat[0:128, rows] = wide.T.astype(jnp.bfloat16)

    def prepare_right(st, h, i):
        rows = pl.ds((4 * h + i) * 128, 128)
        wide = gr[st, h, i].reshape(128, 128).astype(jnp.float32)
        ra[rows, :] = pieces(wide, 3, 0, -0.5)
        rt[:, rows] = wide.T

    def right_arrived(st, h):
        for i in (0, 1, 3, 2):
            if i:
                r_y(st, h, i).wait_recv()
            prepare_right(st, h, i)

    ones = jnp.ones((512, 128), jnp.bfloat16)

    def lefts(ph, c):
        return gl[ph, c // 2, 2 * (c % 2) : 2 * (c % 2) + 2].reshape(512, 128)

    def factor(st, h, c):
        rows, cols = pl.ds(c * 512, 512), pl.ds(h * 512, 512)
        crossed = lax.dot_general(
            jnp.concatenate([lefts(st, c), la[rows, :]], axis=1),
            jnp.concatenate([gr[st, h].reshape(512, 128), ra[cols, :]], axis=1),
            LAST, preferred_element_type=jnp.float32,
        )
        return jnp.exp2(crossed * PAIR_SCALE)

    def produce(st, h, c, slot):
        rows, cols = pl.ds(c * 512, 512), pl.ds(h * 512, 512)
        if st == 0:
            weight = lax.dot_general(
                lefts(2, c), gr[2, h].reshape(512, 128), LAST, preferred_element_type=jnp.float32
            )
            prod[slot] = (weight * kept[rows, cols].astype(jnp.float32)).astype(jnp.bfloat16)
            kept[rows, cols] = weight.astype(jnp.bfloat16)
        else:
            prod[slot] = (kept[rows, cols].astype(jnp.float32) * factor(st, h, c)).astype(jnp.bfloat16)

    def consume(st, h, c, slot, first_h, first_c):
        rows = pl.ds(c * 512, 512)
        product = prod[slot]
        b = gr[st, h].reshape(512, 128)
        left = jnp.dot(product, jnp.concatenate([b, ones], axis=1), preferred_element_type=jnp.float32)
        right = jnp.dot(lat[:, rows], product, preferred_element_type=jnp.float32)
        lacc[rows, :] = left if first_h else lacc[rows, :] + left
        racc[h] = right if first_c else racc[h] + right

    def left_term(st, c):
        rows = pl.ds(c * 512, 512)
        return lacc[rows, 0:128] - lacc[rows, 128:256] * lefts(st, c).astype(jnp.float32)

    def right_out(st, h):
        term = racc[h, 0:128, :] - racc[h, 128:129, :] * rt[:, pl.ds(h * 512, 512)]
        rt[:, pl.ds(h * 512, 128)] = term[:, 0:128]
        for i in (2, 1, 3):
            ty[st, h, i] = term[:, 128 * i : 128 * i + 128].astype(jnp.bfloat16)
            go(c_y(st, h, i))

    def right_home(st, h):
        total = rt[:, pl.ds(h * 512, 128)]
        for i in (1, 3, 2):
            c_y(st, h, i).wait_recv()
            total = total + tyr[st, h, i].astype(jnp.float32)
        tz[st, 2 * h : 2 * h + 2] = total.T.astype(jnp.bfloat16).reshape(2, 64, 128)
        go(c_z(st, h, 0))
        go(c_z(st, h, 1))

    for st in range(STEPS):
        start_right(st, 0)
        if st == 0:
            start_left(st)
        start_right(st, 1)
        if st == 0:
            start_right(2, 0)
            start_left(2)
            start_right(2, 1)
        else:
            sent(8)
        relay_left(st)
        relay_right(st, 1)
        prepare_left(st, 0, 0)
        relay_right(st, 0)
        if st == 0:
            relay_left(2)
            relay_right(2, 1)
            relay_right(2, 0)
        relay_sibling(st)
        for i in (1, 2, 3):
            prepare_left(st, 0, i)
        right_arrived(st, 1)
        for i in range(4):
            l_k(st, i).wait_recv()
            prepare_left(st, 1, i)
        right_arrived(st, 0)
        if st == 0:
            for h in range(2):
                if h == 1:
                    relay_sibling(2)
                for c in range(4):
                    kept[pl.ds(c * 512, 512), pl.ds(h * 512, 512)] = factor(0, h, c).astype(jnp.bfloat16)
            for h in range(2):
                for i in (1, 2, 3):
                    r_y(2, h, i).wait_recv()
            for i in range(4):
                l_k(2, i).wait_recv()

        tiles = [(0, c) for c in (0, 1, 2, 3)] + [(1, c) for c in (3, 2, 1, 0)]
        produce(st, *tiles[0], 0)
        for t, (h, c) in enumerate(tiles):
            consume(st, h, c, t % 2, h == 0, t % 4 == 0)
            if t < 7:
                produce(st, *tiles[t + 1], (t + 1) % 2)
            if t == 3:
                right_out(st, 0)
            if h == 1 and c >= 2:
                ss[st, c - 2] = left_term(st, c).astype(jnp.bfloat16)
                go(b_k(st, c - 2))
            if h == 1 and c == 1:
                b_k(st, 1).wait_recv()
                total = left_term(st, 1) + ssr[st, 1].astype(jnp.float32)
                sx[st, 2:4] = total.astype(jnp.bfloat16).reshape(2, 256, 128)
                go(b_x(st, 2))
                go(b_x(st, 3))
        b_k(st, 0).wait_recv()
        total = left_term(st, 0) + ssr[st, 0].astype(jnp.float32)
        sx[st, 1] = total[256:512].astype(jnp.bfloat16)
        go(b_x(st, 1))
        right_out(st, 1)
        right_home(st, 0)
        total = total[0:256]
        for i in (3, 2, 1):
            b_x(st, i).wait_recv()
            total = total + sxr[st, i].astype(jnp.float32)
        sz[st] = total.astype(jnp.bfloat16).reshape(4, 64, 128)
        for i in (0, 3, 1, 2):
            go(b_z(st, i))
        left = jnp.zeros((64, 128), jnp.float32)
        right_home(st, 1)
        if st + 1 == STEPS:
            sent(6)
        for i in (1, 2, 0, 3):
            b_z(st, i).wait_recv()
            left = left + szr[st, i].astype(jnp.float32)
        if st + 1 < STEPS:
            lv[...] = lv[...] - RATE * (left * GRAD_SCALE)
            own_l[st + 1] = lv[...].astype(jnp.bfloat16)
            start_left(st + 1)
        right = jnp.zeros((64, 128), jnp.float32)
        for h in (1, 0):
            for s in range(2):
                c_z(st, h, s).wait_recv()
                right = right + tzr[st, 2 * h + s].astype(jnp.float32)
        if st + 1 < STEPS:
            rv[...] = rv[...] - RATE * (right * GRAD_SCALE)
            own_r[st + 1] = rv[...].astype(jnp.bfloat16)
        else:
            left, right = left * GRAD_SCALE, right * GRAD_SCALE
            result[0:64, :] = lv[...] - RATE * left
            result[64:128, :] = rv[...] - RATE * right
            result[128:192, :] = left
            result[192:256, :] = right

    sent(0)


def body(left_points, right_points, left_cotangent, right_coefficient):
    f32, bf16 = jnp.float32, jnp.bfloat16
    dma = pltpu.SemaphoreType.DMA
    result = pl.pallas_call(
        pair_kernel,
        name="pairs",
        out_shape=jax.ShapeDtypeStruct((256, 128), f32),
        in_specs=[pl.BlockSpec(memory_space=pl.ANY)] * 4,
        out_specs=pl.BlockSpec(memory_space=pltpu.VMEM),
        scratch_shapes=[
            pltpu.VMEM((64, 128), f32),
            pltpu.VMEM((64, 128), f32),
            pltpu.VMEM((3, 2, 4, 4, 64, 128), bf16),
            pltpu.VMEM((3, 2, 4, 2, 64, 128), bf16),
            pltpu.VMEM((3, 64, 128), bf16),
            pltpu.VMEM((3, 64, 128), bf16),
            pltpu.VMEM((2048, 128), bf16),
            pltpu.VMEM((144, 2048), bf16),
            pltpu.VMEM((1024, 128), bf16),
            pltpu.VMEM((128, 1024), f32),
            pltpu.VMEM((2, 512, 512), bf16),
            pltpu.VMEM((2048, 1024), bf16),
            pltpu.VMEM((2048, 256), f32),
            pltpu.VMEM((2, 144, 512), f32),
            pltpu.VMEM((2, 2, 512, 128), bf16),
            pltpu.VMEM((2, 2, 512, 128), bf16),
            pltpu.VMEM((2, 4, 256, 128), bf16),
            pltpu.VMEM((2, 4, 256, 128), bf16),
            pltpu.VMEM((2, 4, 64, 128), bf16),
            pltpu.VMEM((2, 4, 64, 128), bf16),
            pltpu.VMEM((2, 2, 4, 128, 128), bf16),
            pltpu.VMEM((2, 2, 4, 128, 128), bf16),
            pltpu.VMEM((2, 4, 64, 128), bf16),
            pltpu.VMEM((2, 4, 64, 128), bf16),
            dma((4,)),
            dma((3, 4)), dma((3, 4)),
            dma((3, 4)), dma((3, 4)),
            dma((3, 4)), dma((3, 4)),
            dma((3, 4)), dma((3, 4)),
            dma((3, 8)), dma((3, 8)),
            dma((2, 2)), dma((2, 2)),
            dma((2, 4)), dma((2, 4)),
            dma((2, 4)), dma((2, 4)),
            dma((2, 8)), dma((2, 8)),
            dma((2, 4)), dma((2, 4)),
        ],
        compiler_params=pltpu.CompilerParams(
            collective_id=0, has_side_effects=True, vmem_limit_bytes=64 * 2**20 - 2**16
        ),
    )(left_points, right_points, left_cotangent, right_coefficient)
    return tuple(result[64 * i : 64 * i + 64] for i in range(4))


def solution(mesh):
    spec = P(("row", "col"), None)
    return jax.shard_map(body, mesh=mesh, in_specs=(spec,) * 4, out_specs=(spec,) * 4, check_vma=False)
```

```python
import jax
import jax.numpy as jnp
from jax import lax
from jax.experimental import pallas as pl
from jax.experimental.pallas import tpu as pltpu
from jax.sharding import PartitionSpec as P

STEPS = 2
PAIR_SCALE = 0.0625 * 1.4426950408889634
GRAD_SCALE = 0.0625
RATE = 0.3
MESH = pl.DeviceIdType.MESH
LAST = (((1,), (1,)), ((), ()))

Z_LEFT = (-1, 0, 1, 2)
Z_RIGHT = ((-6, 6), (-2, 2))


def pair_kernel(lp, rp, lc, rc, result, lv, rv, gl, gr, own_r, la, lat, ra, rt, prod, kept, lacc, racc,
                ss, ssr, sx, sxr, sz, szr, ty, tyr, tz, tzr,
                in_sem, lz_s, lz_r, lx_s, lx_r, lk_s, lk_r, rz_s, rz_r, ry_s, ry_r,
                bk_s, bk_r, bx_s, bx_r, bz_s, bz_r, cy_s, cy_r, cz_s, cz_r):
    row, col = lax.axis_index("row"), lax.axis_index("col")
    x, k = row % 4, col % 2
    y = (col // 2) % 4
    z = (col // 8) * 4 + row // 4
    way = 1 - 2 * k

    def at(dx=0, dy=0, dz=0, core=None):
        px, py, pz = (x + dx + 4) % 4, (y + dy + 4) % 4, (z + dz + 16) % 16
        return ((pz % 4) * 4 + px, (pz // 4) * 8 + py * 2 + (k if core is None else core))

    sibling = at(core=1 - k)
    at_x = [None] + [at(dx=i) for i in (1, 2, 3)]
    at_y = [None] + [at(dy=i) for i in (1, 2, 3)]
    z_up = [at(dz=way * o) for o in Z_LEFT]
    z_down = [at(dz=-way * o) for o in Z_LEFT]
    z_far = {o: at(dz=o) for o in (-6, -2, 2, 6)}

    z_on = (at(dz=4), at(dz=-4))

    barrier = pltpu.get_barrier_semaphore()
    partners = [*z_on, z_far[-6], z_far[6], z_far[-2], z_far[2], at(dz=1), at(dz=-1), *at_x[1:], *at_y[1:], sibling]
    for p in partners:
        pl.semaphore_signal(barrier, inc=1, device_id=p, device_id_type=MESH)

    loads = [
        pltpu.make_async_copy(lp, lv, in_sem.at[0]),
        pltpu.make_async_copy(rp, rv, in_sem.at[1]),
        pltpu.make_async_copy(lc, gl.at[2, 0, 0, 1], in_sem.at[2]),
        pltpu.make_async_copy(rc, own_r.at[2], in_sem.at[3]),
    ]
    for c in loads:
        c.start()
    lat[128:144, :] = jnp.ones((16, 2048), jnp.bfloat16)
    for c in loads:
        c.wait()
    gl[0, 0, 0, 1] = lv[...].astype(jnp.bfloat16)
    own_r[0] = rv[...].astype(jnp.bfloat16)
    pl.semaphore_wait(barrier, len(partners))

    def send(src, dst, s, r, device):
        return pltpu.make_async_remote_copy(
            src_ref=src, dst_ref=dst, send_sem=s, recv_sem=r, device_id=device, device_id_type=MESH
        )

    pending = []

    def go(copy):
        copy.start()
        pending.append(copy)

    def sent(keep):
        for copy in pending[: len(pending) - keep]:
            copy.wait_send()
        del pending[: len(pending) - keep]

    def l_z(ph, i):
        return send(gl.at[ph, 0, 0, 1], gl.at[ph, 0, 0, i], lz_s.at[ph, i], lz_r.at[ph, i], z_down[i])

    def l_x(ph, i):
        return send(gl.at[ph, 0, 0], gl.at[ph, 0, i], lx_s.at[ph, i], lx_r.at[ph, i], at_x[i])

    def l_k(ph, i):
        return send(gl.at[ph, 0, i], gl.at[ph, 1, i], lk_s.at[ph, i], lk_r.at[ph, i], sibling)

    def r_z(ph, h, s):
        n = 2 * h + s
        if h == 0:
            return send(gr.at[ph, 1, 0, s], gr.at[ph, 0, 0, s], rz_s.at[ph, n], rz_r.at[ph, n], z_on[s])
        return send(own_r.at[ph], gr.at[ph, h, 0, s], rz_s.at[ph, n], rz_r.at[ph, n], z_far[-Z_RIGHT[h][s]])

    def r_y(ph, h, i):
        n = 4 * h + i
        return send(gr.at[ph, h, 0], gr.at[ph, h, i], ry_s.at[ph, n], ry_r.at[ph, n], at_y[i])

    def gather_start(ph):
        go(r_z(ph, 1, 0))
        go(r_z(ph, 1, 1))
        for i in (3, 0, 2):
            go(l_z(ph, i))

    def pass_on(ph):
        for s in range(2):
            r_z(ph, 1, s).wait_recv()
            go(r_z(ph, 0, s))

    def relay_left(ph):
        for i in (0, 2, 3):
            l_z(ph, i).wait_recv()
        for i in (2, 1, 3):
            go(l_x(ph, i))
        go(l_k(ph, 0))

    def relay_right(ph, h):
        if h == 0:
            r_z(ph, 0, 0).wait_recv()
            r_z(ph, 0, 1).wait_recv()
        for i in (2, 1, 3):
            go(r_y(ph, h, i))

    def relay_sibling(ph):
        for i in (1, 3, 2):
            l_x(ph, i).wait_recv()
            go(l_k(ph, i))

    def b_k(st, c):
        return send(ss.at[st, c], ssr.at[st, c], bk_s.at[st, c], bk_r.at[st, c], sibling)

    def b_x(st, i):
        return send(sx.at[st, i], sxr.at[st, i], bx_s.at[st, i], bx_r.at[st, i], at_x[4 - i])

    def b_z(st, i):
        return send(sz.at[st, i], szr.at[st, i], bz_s.at[st, i], bz_r.at[st, i], z_up[i])

    def c_y(st, h, i):
        n = 4 * h + i
        return send(ty.at[st, h, i], tyr.at[st, h, i], cy_s.at[st, n], cy_r.at[st, n], at_y[4 - i])

    def c_z(st, h, s):
        n = 2 * h + s
        return send(tz.at[st, n], tzr.at[st, n], cz_s.at[st, n], cz_r.at[st, n], z_far[Z_RIGHT[h][s]])

    def pieces(v, own, other, scale):
        norm = jnp.sum(v * v, axis=1, keepdims=True)
        hi = norm.astype(jnp.bfloat16).astype(jnp.float32)
        rest = norm - hi
        mid = rest.astype(jnp.bfloat16).astype(jnp.float32)
        low = rest - mid
        lane = lax.broadcasted_iota(jnp.int32, v.shape, 1)
        out = jnp.where((lane >= other) & (lane < other + 3), scale, jnp.zeros_like(v))
        out = jnp.where(lane == own, scale * hi, out)
        out = jnp.where(lane == own + 1, scale * mid, out)
        return jnp.where(lane == own + 2, scale * low, out).astype(jnp.bfloat16)

    def prepare_left(st, m, i):
        rows = pl.ds((4 * m + i) * 256, 256)
        wide = gl[st, m, i].reshape(256, 128).astype(jnp.float32)
        la[rows, :] = pieces(wide, 0, 3, 1.0)
        lat[0:128, rows] = wide.T.astype(jnp.bfloat16)

    def prepare_right(st, h, i):
        rows = pl.ds((4 * h + i) * 128, 128)
        wide = gr[st, h, i].reshape(128, 128).astype(jnp.float32)
        ra[rows, :] = pieces(wide, 3, 0, -0.5)
        rt[:, rows] = wide.T

    ones = jnp.ones((512, 128), jnp.bfloat16)

    def lefts(ph, c):
        return gl[ph, c // 2, 2 * (c % 2) : 2 * (c % 2) + 2].reshape(512, 128)

    def factor(st, h, c):
        rows, cols = pl.ds(c * 512, 512), pl.ds(h * 512, 512)
        crossed = lax.dot_general(
            jnp.concatenate([lefts(st, c), la[rows, :]], axis=1),
            jnp.concatenate([gr[st, h].reshape(512, 128), ra[cols, :]], axis=1),
            LAST, preferred_element_type=jnp.float32,
        )
        return jnp.exp2(crossed * PAIR_SCALE)

    def produce(st, h, c, slot):
        rows, cols = pl.ds(c * 512, 512), pl.ds(h * 512, 512)
        if st == 0:
            weight = lax.dot_general(
                lefts(2, c), gr[2, h].reshape(512, 128), LAST, preferred_element_type=jnp.float32
            )
            prod[slot] = (weight * kept[rows, cols].astype(jnp.float32)).astype(jnp.bfloat16)
            kept[rows, cols] = weight.astype(jnp.bfloat16)
        else:
            prod[slot] = (kept[rows, cols].astype(jnp.float32) * factor(st, h, c)).astype(jnp.bfloat16)

    def consume(st, h, c, slot, first_h, first_c):
        rows = pl.ds(c * 512, 512)
        product = prod[slot]
        b = gr[st, h].reshape(512, 128)
        left = jnp.dot(product, jnp.concatenate([b, ones], axis=1), preferred_element_type=jnp.float32)
        right = jnp.dot(lat[:, rows], product, preferred_element_type=jnp.float32)
        lacc[rows, :] = left if first_h else lacc[rows, :] + left
        racc[h] = right if first_c else racc[h] + right

    def left_term(st, c):
        rows = pl.ds(c * 512, 512)
        return lacc[rows, 0:128] - lacc[rows, 128:256] * lefts(st, c).astype(jnp.float32)

    def right_out(st, h):
        term = racc[h, 0:128, :] - racc[h, 128:129, :] * rt[:, pl.ds(h * 512, 512)]
        rt[:, pl.ds(h * 512, 128)] = term[:, 0:128]
        for i in (2, 1, 3):
            ty[st, h, i] = term[:, 128 * i : 128 * i + 128].astype(jnp.bfloat16)
            go(c_y(st, h, i))

    def right_home(st, h):
        total = rt[:, pl.ds(h * 512, 128)]
        for i in (1, 3, 2):
            c_y(st, h, i).wait_recv()
            total = total + tyr[st, h, i].astype(jnp.float32)
        tz[st, 2 * h : 2 * h + 2] = total.T.astype(jnp.bfloat16).reshape(2, 64, 128)
        go(c_z(st, h, 0))
        go(c_z(st, h, 1))

    for st in range(STEPS):
        gather_start(st)
        if st == 0:
            gather_start(2)
        else:
            sent(5)
        pass_on(st)
        if st == 0:
            pass_on(2)
        relay_left(st)
        relay_right(st, 1)
        prepare_left(st, 0, 0)
        relay_right(st, 0)
        if st == 0:
            relay_left(2)
            relay_right(2, 1)
            relay_right(2, 0)
        relay_sibling(st)
        for i in (1, 2, 3):
            prepare_left(st, 0, i)
        for h in (1, 0):
            for i in range(4):
                if i:
                    r_y(st, h, i).wait_recv()
                prepare_right(st, h, i)
        if st == 0:
            relay_sibling(2)
        for i in range(4):
            l_k(st, i).wait_recv()
            prepare_left(st, 1, i)
        if st == 0:
            for h in range(2):
                for c in range(4):
                    kept[pl.ds(c * 512, 512), pl.ds(h * 512, 512)] = factor(0, h, c).astype(jnp.bfloat16)
            for h in range(2):
                for i in (1, 2, 3):
                    r_y(2, h, i).wait_recv()
            for i in range(4):
                l_k(2, i).wait_recv()

        tiles = [(0, c) for c in (0, 1, 2, 3)] + [(1, c) for c in (3, 2, 1, 0)]
        produce(st, *tiles[0], 0)
        for t, (h, c) in enumerate(tiles):
            consume(st, h, c, t % 2, h == 0, t % 4 == 0)
            if t < 7:
                produce(st, *tiles[t + 1], (t + 1) % 2)
            if t == 3:
                right_out(st, 0)
            if h == 1 and c >= 2:
                ss[st, c - 2] = left_term(st, c).astype(jnp.bfloat16)
                go(b_k(st, c - 2))
            if h == 1 and c == 1:
                b_k(st, 1).wait_recv()
                total = left_term(st, 1) + ssr[st, 1].astype(jnp.float32)
                sx[st, 2:4] = total.astype(jnp.bfloat16).reshape(2, 256, 128)
                go(b_x(st, 2))
                go(b_x(st, 3))
        b_k(st, 0).wait_recv()
        total = left_term(st, 0) + ssr[st, 0].astype(jnp.float32)
        sx[st, 1] = total[256:512].astype(jnp.bfloat16)
        go(b_x(st, 1))
        right_out(st, 1)
        right_home(st, 0)
        total = total[0:256]
        for i in (3, 2, 1):
            b_x(st, i).wait_recv()
            total = total + sxr[st, i].astype(jnp.float32)
        sz[st] = total.astype(jnp.bfloat16).reshape(4, 64, 128)
        for i in (3, 0, 2):
            go(b_z(st, i))
        left = total[64:128]
        right_home(st, 1)
        if st + 1 == STEPS:
            sent(5)
        for i in (0, 2, 3):
            b_z(st, i).wait_recv()
            left = left + szr[st, i].astype(jnp.float32)
        if st + 1 < STEPS:
            lv[...] = lv[...] - RATE * (left * GRAD_SCALE)
            gl[st + 1, 0, 0, 1] = lv[...].astype(jnp.bfloat16)
        right = jnp.zeros((64, 128), jnp.float32)
        for h in (1, 0):
            for s in range(2):
                c_z(st, h, s).wait_recv()
                right = right + tzr[st, 2 * h + s].astype(jnp.float32)
        if st + 1 < STEPS:
            rv[...] = rv[...] - RATE * (right * GRAD_SCALE)
            own_r[st + 1] = rv[...].astype(jnp.bfloat16)
        else:
            left, right = left * GRAD_SCALE, right * GRAD_SCALE
            result[0:64, :] = lv[...] - RATE * left
            result[64:128, :] = rv[...] - RATE * right
            result[128:192, :] = left
            result[192:256, :] = right

    sent(0)


def body(left_points, right_points, left_cotangent, right_coefficient):
    f32, bf16 = jnp.float32, jnp.bfloat16
    dma = pltpu.SemaphoreType.DMA
    result = pl.pallas_call(
        pair_kernel,
        name="pairs",
        out_shape=jax.ShapeDtypeStruct((256, 128), f32),
        in_specs=[pl.BlockSpec(memory_space=pl.ANY)] * 4,
        out_specs=pl.BlockSpec(memory_space=pltpu.VMEM),
        scratch_shapes=[
            pltpu.VMEM((64, 128), f32),
            pltpu.VMEM((64, 128), f32),
            pltpu.VMEM((3, 2, 4, 4, 64, 128), bf16),
            pltpu.VMEM((3, 2, 4, 2, 64, 128), bf16),
            pltpu.VMEM((3, 64, 128), bf16),
            pltpu.VMEM((2048, 128), bf16),
            pltpu.VMEM((144, 2048), bf16),
            pltpu.VMEM((1024, 128), bf16),
            pltpu.VMEM((128, 1024), f32),
            pltpu.VMEM((2, 512, 512), bf16),
            pltpu.VMEM((2048, 1024), bf16),
            pltpu.VMEM((2048, 256), f32),
            pltpu.VMEM((2, 144, 512), f32),
            pltpu.VMEM((2, 2, 512, 128), bf16),
            pltpu.VMEM((2, 2, 512, 128), bf16),
            pltpu.VMEM((2, 4, 256, 128), bf16),
            pltpu.VMEM((2, 4, 256, 128), bf16),
            pltpu.VMEM((2, 4, 64, 128), bf16),
            pltpu.VMEM((2, 4, 64, 128), bf16),
            pltpu.VMEM((2, 2, 4, 128, 128), bf16),
            pltpu.VMEM((2, 2, 4, 128, 128), bf16),
            pltpu.VMEM((2, 4, 64, 128), bf16),
            pltpu.VMEM((2, 4, 64, 128), bf16),
            dma((4,)),
            dma((3, 4)), dma((3, 4)),
            dma((3, 4)), dma((3, 4)),
            dma((3, 4)), dma((3, 4)),
            dma((3, 4)), dma((3, 4)),
            dma((3, 8)), dma((3, 8)),
            dma((2, 2)), dma((2, 2)),
            dma((2, 4)), dma((2, 4)),
            dma((2, 4)), dma((2, 4)),
            dma((2, 8)), dma((2, 8)),
            dma((2, 4)), dma((2, 4)),
        ],
        compiler_params=pltpu.CompilerParams(
            collective_id=0, has_side_effects=True, vmem_limit_bytes=64 * 2**20 - 2**16
        ),
    )(left_points, right_points, left_cotangent, right_coefficient)
    return tuple(result[64 * i : 64 * i + 64] for i in range(4))


def solution(mesh):
    spec = P(("row", "col"), None)
    return jax.shard_map(body, mesh=mesh, in_specs=(spec,) * 4, out_specs=(spec,) * 4, check_vma=False)
```
